256 devices in a mesh: dp: 64 (over z, x, y_hi), tok: 4 (over y_lo, core).
Axes of the slice: x: 4, y: 4 (y_hi: 2, y_lo: 2; y = y_hi * 2 + y_lo), z: 8, core: 2. Of those that a mesh axis runs over, the one named last changes fastest.
Arguments:
- acts: bfloat16 [128, 512, 14336], P('dp', 'tok'), may hold values from -30 to 30
- grads: bfloat16 [128, 512, 4096], P('dp', 'tok'), may hold values from -30 to 30
- lengths: int32 [128], P('dp'), may hold values from 1 to 512, as said below
- domains: int32 [128, 1], replicated, may hold values from 0 to 15
- hash_salts: int32 [2], replicated, may hold values from 0 to 46336
Outputs:
- example_grads: bfloat16 [128, 65536], P('dp', 'tok')
- kernel: float32 [16, 16], replicated
The draws below stay inside these ranges and needn't reach their ends.
Inputs may be any that keep to these rules, and one draw needn't show every extreme that they name: `lengths`: some example has all 512 slots live in every draw. `domains`: every domain holds at least one example.
All inputs are finite; a program needn't handle non-finite values.
Results may differ from the reference program's by a relative error of at most 0.0057.
Values may be sent and summed in bfloat16 or wider, within the bound.
A program may use at most 128 MiB of HBM per device.

```python
import math
import jax
import jax.numpy as jnp
from jax import lax

D = 4096
FF = 14336
KX = 256
KG = 256
LEN = 512
DOMAINS = 16
EXAMPLES = 128


def scaled_field(key, shape):
    key_base, key_rows, key_cols = jax.random.split(key, 3)
    row_scale = jnp.exp(jax.random.uniform(key_rows, (shape[0], shape[1], 1), minval=math.log(0.3), maxval=math.log(3.0)))
    col_scale = jnp.exp(jax.random.uniform(key_cols, (shape[2],), minval=math.log(0.5), maxval=math.log(2.0)))
    base = jnp.clip(jax.random.normal(key_base, shape), -4.0, 4.0)
    return (base * row_scale * col_scale).astype(jnp.float32)


def draw_acts(key, part):
    field = scaled_field(jax.random.fold_in(key, 11), (EXAMPLES, LEN, FF))
    return field.astype(jnp.bfloat16)


def draw_grads(key, part):
    field = scaled_field(jax.random.fold_in(key, 23), (EXAMPLES, LEN, D))
    return field.astype(jnp.bfloat16)


def draw_lengths(key, part):
    key_base, key_shrink, key_pick = jax.random.split(jax.random.fold_in(key, 37), 3)
    base = jax.random.randint(key_base, (EXAMPLES,), 1, LEN + 1)
    shrink = jax.random.randint(key_shrink, (EXAMPLES,), 1, 5)
    counts = jnp.maximum(base // shrink, 1)
    pick = jax.random.randint(key_pick, (), 0, EXAMPLES)
    index = jnp.arange(EXAMPLES, dtype=jnp.int32)
    return jnp.where(index == pick, LEN, counts).astype(jnp.int32)


def picks_of(rng, rows, amount, top, lift):
    ranking = jax.random.permutation(jax.random.fold_in(rng, 1), amount)
    favour = ranking
    for power in range(3):
        favour = favour * favour // amount
    favour = favour * lift // amount
    chance = jax.random.randint(jax.random.fold_in(rng, 2), (rows, amount), 0, 4096) + favour
    holders = jax.random.permutation(jax.random.fold_in(rng, 3), rows)[jnp.arange(amount) % rows]
    chance = jnp.where(jnp.arange(rows)[:, None] == holders[None, :], 1 << 14, chance)
    priority = chance * amount + jnp.arange(amount)
    return lax.top_k(priority.astype(jnp.int32), top)[1].astype(jnp.int32)


def setup_inputs(seed: int = 0) -> dict:
    key_of = jax.random.split(jax.random.key(seed), 6)
    acts = draw_acts(jax.random.fold_in(key_of[5], 71), 0)
    grads = draw_grads(jax.random.fold_in(key_of[5], 71), 0)
    lengths = draw_lengths(jax.random.fold_in(key_of[5], 71), 0)
    domains = picks_of(key_of[3], EXAMPLES, DOMAINS, 1, 512)
    hash_salts = jax.random.randint(key_of[4], (2,), 0, 46337).astype(jnp.int32)
    return {"acts": acts, "grads": grads, "lengths": lengths, "domains": domains, "hash_salts": hash_salts}


def sign_table(rows, cols, salt_value):
    row_idx = lax.broadcasted_iota(jnp.int32, (rows, cols), 0)
    col_idx = lax.broadcasted_iota(jnp.int32, (rows, cols), 1)
    first = (row_idx * 7919 + col_idx * 6007 + salt_value) % 46337
    second = (first * first + 3 * row_idx + col_idx) % 46337
    third = (second * second + salt_value) % 46337
    return jnp.where(third % 2 == 1, 1.0, -1.0).astype(jnp.bfloat16)

def reference(acts, grads, lengths, domains, hash_salts):
    table_x = sign_table(FF, KX, hash_salts[0])
    table_g = sign_table(D, KG, hash_salts[1])

    def one_example(items):
        act, grad, length = items
        live = (lax.broadcasted_iota(jnp.int32, (LEN, 1), 0) < length).astype(jnp.float32)
        proj_x = (jnp.dot(act, table_x, preferred_element_type=jnp.float32) * (live / math.sqrt(FF))).astype(jnp.bfloat16)
        proj_g = (jnp.dot(grad, table_g, preferred_element_type=jnp.float32) * (live / math.sqrt(D))).astype(jnp.bfloat16)
        outer = jnp.einsum('tg,tk->gk', proj_g.astype(jnp.float32), proj_x.astype(jnp.float32), precision=lax.Precision.HIGHEST)
        return outer.reshape(KG * KX)
    summed = lax.map(one_example, (acts, grads, lengths))
    example_grads = (summed / math.sqrt(LEN)).astype(jnp.bfloat16)
    onehot = (domains[:, 0][:, None] == lax.broadcasted_iota(jnp.int32, (domains.shape[0], DOMAINS), 1)).astype(jnp.float32)
    domain_sums = jnp.dot(onehot.T, example_grads.astype(jnp.float32), precision=lax.Precision.HIGHEST)
    kernel = jnp.dot(domain_sums, domain_sums.T, precision=lax.Precision.HIGHEST) / (16.0 * KX * KG)
    return (example_grads, kernel)
```

```python
import functools
import math

import jax
import jax.numpy as jnp
import numpy as np
from jax import lax
from jax.experimental import pallas as pl
from jax.experimental.pallas import tpu as pltpu
from jax.sharding import PartitionSpec as P

KX = 256
KG = 256
LEN = 512
DOMAINS = 16
MESH = pl.DeviceIdType.MESH

PR = 46337
INV2 = (PR + 1) // 2
HALF_ROOT = 19963
UNIT = HALF_ROOT * pow(2, 16, PR) % PR
BACK = pow(pow(2, 32, PR), -1, PR)
TURN = (BACK * 2**32 - 1) // PR
STEP_WHOLE = 2**32 // PR
STEP_REST = 2**32 % PR
BIAS = 46343
ROWS = 1024
PAIR = 2 * ROWS


def centered(value):
    value = value % PR
    return value - PR if value > PR // 2 else value


def row_matrix(chunks):
    local = np.arange(ROWS)
    b, a, z = local // 128, local // 8 % 16, local % 8
    out = np.zeros((ROWS, 128), np.float32)
    for offset, digit in ((0, b), (8, b), (16, a), (32, a), (48, z), (56, z)):
        out[local, offset + digit] = 1.0
    for g in range(chunks):
        cross = (ROWS * g + 128 * b) * (8 * a + z) + 8 * a * z
        value = (2 * UNIT * 7919 * 7919 % PR) * (cross % PR) % PR
        value = np.where(value > PR // 2, value - PR, value)
        high = np.round(value / 256)
        out[:, 64 + 2 * g] = high
        out[:, 65 + 2 * g] = value - 256 * high
    return out


def reduced(value):
    return value - float(PR) * jnp.round(value * (1.0 / PR))


def digits(value):
    high = jnp.round(value * (1.0 / 256))
    return high, value - 256.0 * high


def product(left, right):
    high, low = digits(left)
    return reduced(high * reduced(256.0 * right) + low * right)


def iotas(rows):
    row = lax.broadcasted_iota(jnp.int32, (rows, KX), 0).astype(jnp.float32)
    col = lax.broadcasted_iota(jnp.int32, (rows, KX), 1).astype(jnp.float32)
    return row, col


def linear_terms(rows, unit, beta):
    row, _ = iotas(rows)
    slope = reduced(float(centered(2 * UNIT * 7919 * unit)) * row)
    square = reduced(float(centered(UNIT * 7919 * 7919 * unit * unit)) * (row * row))
    line = reduced(float(centered(3 * UNIT * unit)) * row)
    return reduced(product(slope, beta) + square + line)


def column_tables(salt, chunks, first, rall):
    salt = salt.astype(jnp.float32)

    def beta(rows):
        _, col = iotas(rows)
        return reduced(6007.0 * col + salt)

    row, col = iotas(8 * chunks)
    inner = reduced(reduced(float(centered(7919 * 128)) * row) + beta(8 * chunks))
    value = reduced(product(inner, inner) + (384.0 * row + col))
    base_high, base_low = digits(product(jnp.full_like(value, float(centered(UNIT))), value))
    mid_high, mid_low = digits(linear_terms(16, 8, beta(16)))
    low_high, low_low = digits(linear_terms(8, 1, beta(8)))
    pick = lax.broadcasted_iota(jnp.int32, (64, KX), 0)
    for g in range(chunks):
        cross = jnp.where(pick == 2 * g, 256.0, jnp.where(pick == 2 * g + 1, 1.0, 0.0))
        rall[first + g] = jnp.concatenate(
            [
                256.0 * base_high[8 * g : 8 * g + 8],
                base_low[8 * g : 8 * g + 8],
                256.0 * mid_high,
                mid_low,
                256.0 * low_high,
                low_low,
                cross,
            ],
            axis=0,
        ).astype(jnp.bfloat16)


def salt_turn(salt):
    half = jnp.where(salt % 2 == 1, (salt + PR) // 2, salt // 2)
    whole = half * jnp.int32(STEP_WHOLE - 2**32 if STEP_WHOLE >= 2**31 else STEP_WHOLE)
    return whole + (half * STEP_REST) // PR + BIAS


def kernel(
    width_x,
    width_g,
    lengths_ref,
    salts_ref,
    acts_ref,
    grads_ref,
    rows_ref,
    domains_ref,
    eg_ref,
    out_ref,
    xbuf,
    table,
    rall,
    acc,
    part,
    tok_send,
    tok_slot,
    msg,
    dom_slot,
    sums,
    sum_slot,
    gram_b,
    gram_a,
    in_sem,
    tok_ss,
    tok_rs,
    msg_ss,
    msg_rs,
    sum_ss,
    sum_rs,
    gb_ss,
    gb_rs,
    ga_ss,
    ga_rs,
):
    dp, tok = lax.axis_index("dp"), lax.axis_index("tok")
    z, x, yh = dp // 8, (dp // 2) % 4, dp % 2
    ia, ib = z * 2 + yh, x * 4 + tok

    def peer_a(i):
        return ((i // 2) * 8 + x * 2 + i % 2, tok)

    def peer_b(i):
        return (z * 8 + (i // 4) * 2 + yh, i % 4)

    n_g, n_x = width_g // PAIR, width_x // PAIR
    n = n_g + n_x
    loads = [
        pltpu.make_async_copy(grads_ref.at[:, pl.ds(c * PAIR, PAIR)], xbuf.at[c], in_sem.at[c])
        for c in range(n_g)
    ] + [
        pltpu.make_async_copy(
            acts_ref.at[:, pl.ds(c * PAIR, PAIR)], xbuf.at[n_g + c], in_sem.at[n_g + c]
        )
        for c in range(n_x)
    ]
    for load in loads:
        load.start()

    barrier = pltpu.get_barrier_semaphore()

    def greet(k, _):
        pl.semaphore_signal(barrier, inc=1, device_id=peer_a((ia + k) % 16), device_id_type=MESH)
        pl.semaphore_signal(barrier, inc=1, device_id=peer_b((ib + k) % 16), device_id_type=MESH)
        return 0

    lax.fori_loop(1, 16, greet, 0)

    salt_x, salt_g = salts_ref[0], salts_ref[1]
    column_tables(salt_g, 2 * n_g, 0, rall)
    column_tables(salt_x, 2 * n_x, 2 * n_g, rall)
    turn_x, turn_g = salt_turn(salt_x), salt_turn(salt_g)
    acc[...] = jnp.zeros_like(acc)

    def make_table(c, slot):
        turn = jnp.where(c < n_g, turn_g, turn_x)
        for half in range(2):
            value = jnp.dot(rows_ref[...], rall[2 * c + half], preferred_element_type=jnp.float32)
            small = (jnp.abs(value) - float(PR)).astype(jnp.int32)
            angle = small * small * jnp.int32(TURN - 2**32) + turn
            sign = jnp.where(angle < 0, 1.0, -1.0).astype(jnp.bfloat16)
            table[slot, pl.ds(half * ROWS, ROWS), :] = sign

    def project(c, slot):
        which = jnp.where(c < n_g, 0, 1)
        pltpu.make_async_copy(acts_ref.at[:, pl.ds(0, PAIR)], xbuf.at[c], in_sem.at[c]).wait()
        acc[which] += jnp.dot(xbuf[c], table[slot], preferred_element_type=jnp.float32)

    make_table(0, 0)

    def step(c, _):
        slot = lax.rem(c, 2)
        project(c, slot)
        make_table(c + 1, 1 - slot)
        return 0

    lax.fori_loop(0, n - 1, step, 0)
    project(n - 1, (n - 1) % 2)

    seg = acc.shape[1] // 2
    position = tok * seg + lax.broadcasted_iota(jnp.int32, (seg, KX), 0)
    for e in range(2):
        live = (position < lengths_ref[e]).astype(jnp.float32)
        rows = pl.ds(e * seg, seg)
        proj_g = (acc[0, rows, :] * (live / math.sqrt(width_g))).astype(jnp.bfloat16)
        proj_x = (acc[1, rows, :] * (live / math.sqrt(width_x))).astype(jnp.bfloat16)
        outer = lax.dot_general(
            proj_g, proj_x, (((0,), (0,)), ((), ())), preferred_element_type=jnp.float32
        )
        for q in range(4):
            block = outer[64 * q : 64 * q + 64]
            part[q, e] = block
            tok_send[q, e] = block.astype(jnp.bfloat16)

    pl.semaphore_wait(barrier, 30)

    def tok_copy(k):
        to = (tok + k) % 4
        return pltpu.make_async_remote_copy(
            src_ref=tok_send.at[to],
            dst_ref=tok_slot.at[tok],
            send_sem=tok_ss.at[k],
            recv_sem=tok_rs.at[tok],
            device_id=(dp, to),
            device_id_type=MESH,
        )

    def tok_arrival(k):
        source = (tok + k) % 4
        return pltpu.make_async_remote_copy(
            src_ref=tok_send.at[source],
            dst_ref=tok_slot.at[source],
            send_sem=tok_ss.at[k],
            recv_sem=tok_rs.at[source],
            device_id=(dp, source),
            device_id_type=MESH,
        )

    for k in range(1, 4):
        tok_copy(k).start()

    lane = lax.broadcasted_iota(jnp.int32, (128, 256), 1)
    row = lax.broadcasted_iota(jnp.int32, (128, 256), 0)
    source = lane // 16
    example = 2 * ((source // 2) * 8 + x * 2 + source % 2) + (lane // 8) % 2
    chosen = (row == example).astype(jnp.bfloat16)
    labels = jnp.broadcast_to(domains_ref[...], (8, 128)).astype(jnp.float32).astype(jnp.bfloat16)
    label = jnp.dot(labels, chosen, preferred_element_type=jnp.float32)[0:1].astype(jnp.int32)
    hot = ((label == row % 16) & (row // 16 == lane % 8)).astype(jnp.float32).astype(jnp.bfloat16)

    for k in range(1, 4):
        tok_arrival(k).wait_recv()
    total = part[tok]
    for k in range(1, 4):
        total = total + tok_slot[(tok + k) % 4].astype(jnp.float32)
    total = total / math.sqrt(LEN)
    eg_ref[...] = total.astype(jnp.bfloat16)
    for t in range(16):
        r, c = 8 * (t // 2), 128 * (t % 2)
        msg[t] = jnp.concatenate(
            [total[0, r : r + 8, c : c + 128], total[1, r : r + 8, c : c + 128]], axis=0
        ).astype(jnp.bfloat16)

    def msg_copy(k):
        to = (ia + k) % 16
        return pltpu.make_async_remote_copy(
            src_ref=msg.at[to],
            dst_ref=dom_slot.at[ia],
            send_sem=msg_ss.at[k],
            recv_sem=msg_rs.at[ia],
            device_id=peer_a(to),
            device_id_type=MESH,
        )

    def msg_arrival(k):
        source = (ia + k) % 16
        return pltpu.make_async_remote_copy(
            src_ref=msg.at[source],
            dst_ref=dom_slot.at[source],
            send_sem=msg_ss.at[k],
            recv_sem=msg_rs.at[source],
            device_id=peer_a(source),
            device_id_type=MESH,
        )

    def each(count, action):
        def once(k, _):
            action(k)
            return 0

        lax.fori_loop(1, count, once, 0)

    each(16, lambda k: msg_copy(k).start())
    dom_slot[ia] = msg[ia]
    each(16, lambda k: msg_arrival(k).wait_recv())
    held = dom_slot[...].reshape(256, 128)
    domain_part = jnp.dot(hot, held, preferred_element_type=jnp.float32)
    for q in range(4):
        sums[q] = domain_part[32 * q : 32 * q + 32]

    def sum_copy(k):
        to = (x + k) % 4
        return pltpu.make_async_remote_copy(
            src_ref=sums.at[to],
            dst_ref=sum_slot.at[x],
            send_sem=sum_ss.at[k],
            recv_sem=sum_rs.at[x],
            device_id=(z * 8 + to * 2 + yh, tok),
            device_id_type=MESH,
        )

    def sum_arrival(k):
        source = (x + k) % 4
        return pltpu.make_async_remote_copy(
            src_ref=sums.at[source],
            dst_ref=sum_slot.at[source],
            send_sem=sum_ss.at[k],
            recv_sem=sum_rs.at[source],
            device_id=(z * 8 + source * 2 + yh, tok),
            device_id_type=MESH,
        )

    for k in range(1, 4):
        sum_copy(k).start()
    sum_slot[x] = sums[x]
    for k in range(1, 4):
        sum_arrival(k).wait_recv()
    share = (sum_slot[0] + sum_slot[1]) + (sum_slot[2] + sum_slot[3])
    wide = jnp.zeros((16, 128), jnp.float32)
    for r in range(2):
        own = share[16 * r : 16 * r + 16]
        wide = wide + lax.dot_general(
            own,
            jnp.concatenate([own] * 8, axis=0),
            (((1,), (1,)), ((), ())),
            precision=lax.Precision.HIGHEST,
            preferred_element_type=jnp.float32,
        )
    on_diagonal = (
        lax.broadcasted_iota(jnp.int32, (16, 128), 1) // 16
        == lax.broadcasted_iota(jnp.int32, (16, 128), 0) % 8
    )
    wide = jnp.where(on_diagonal, wide, 0.0)
    flat = jnp.concatenate(
        [jnp.sum(wide[:8], axis=0, keepdims=True), jnp.sum(wide[8:], axis=0, keepdims=True)], axis=0
    )

    def gram_copy(slots, sends, receives, me, peer, k, to):
        return pltpu.make_async_remote_copy(
            src_ref=slots.at[me],
            dst_ref=slots.at[to],
            send_sem=sends.at[k],
            recv_sem=receives.at[to],
            device_id=peer((me + k) % 16),
            device_id_type=MESH,
        )

    for slots, sends, receives, me, peer in (
        (gram_b, gb_ss, gb_rs, ib, peer_b),
        (gram_a, ga_ss, ga_rs, ia, peer_a),
    ):
        slots[me] = flat
        copy = functools.partial(gram_copy, slots, sends, receives, me, peer)
        each(16, lambda k: copy(k, me).start())
        each(16, lambda k: copy(k, (me + k) % 16).wait_recv())
        flat = jnp.sum(slots[...], axis=0)

    spread = jnp.concatenate(
        [jnp.broadcast_to(flat[0:1], (8, 128)), jnp.broadcast_to(flat[1:2], (8, 128))], axis=0
    )
    spread = jnp.where(on_diagonal, spread, 0.0)
    fold = (
        lax.broadcasted_iota(jnp.int32, (128, 16), 0) % 16
        == lax.broadcasted_iota(jnp.int32, (128, 16), 1)
    ).astype(jnp.float32)
    out_ref[...] = jnp.dot(
        spread, fold, precision=lax.Precision.HIGHEST, preferred_element_type=jnp.float32
    ) / (16.0 * KX * KG)

    for k in range(1, 4):
        tok_copy(k).wait_send()
        sum_copy(k).wait_send()
    each(16, lambda k: msg_copy(k).wait_send())
    each(16, lambda k: gram_copy(gram_b, gb_ss, gb_rs, ib, peer_b, k, ib).wait_send())
    each(16, lambda k: gram_copy(gram_a, ga_ss, ga_rs, ia, peer_a, k, ia).wait_send())


def body(acts, grads, lengths, domains, hash_salts):
    ex_dev, seg, width_x = acts.shape
    width_g = grads.shape[2]
    tokens = ex_dev * seg
    chunks = (width_x + width_g) // PAIR
    rows = jnp.asarray(row_matrix(width_x // ROWS), jnp.bfloat16)
    dma = pltpu.SemaphoreType.DMA
    grads_out, gram = pl.pallas_call(
        functools.partial(kernel, width_x, width_g),
        out_shape=(
            jax.ShapeDtypeStruct((ex_dev, 64, KX), jnp.bfloat16),
            jax.ShapeDtypeStruct((DOMAINS, DOMAINS), jnp.float32),
        ),
        in_specs=[
            pl.BlockSpec(memory_space=pltpu.SMEM),
            pl.BlockSpec(memory_space=pltpu.SMEM),
            pl.BlockSpec(memory_space=pl.ANY),
            pl.BlockSpec(memory_space=pl.ANY),
            pl.BlockSpec(memory_space=pltpu.VMEM),
            pl.BlockSpec(memory_space=pltpu.VMEM),
        ],
        out_specs=(
            pl.BlockSpec(memory_space=pltpu.VMEM),
            pl.BlockSpec(memory_space=pltpu.VMEM),
        ),
        scratch_shapes=[
            pltpu.VMEM((chunks, tokens, PAIR), jnp.bfloat16),
            pltpu.VMEM((2, PAIR, KX), jnp.bfloat16),
            pltpu.VMEM((2 * chunks, 128, KX), jnp.bfloat16),
            pltpu.VMEM((2, tokens, KX), jnp.float32),
            pltpu.VMEM((4, 2, 64, KX), jnp.float32),
            pltpu.VMEM((4, 2, 64, KX), jnp.bfloat16),
            pltpu.VMEM((4, 2, 64, KX), jnp.bfloat16),
            pltpu.VMEM((16, 16, 128), jnp.bfloat16),
            pltpu.VMEM((16, 16, 128), jnp.bfloat16),
            pltpu.VMEM((4, 32, 128), jnp.float32),
            pltpu.VMEM((4, 32, 128), jnp.float32),
            pltpu.VMEM((16, 2, 128), jnp.float32),
            pltpu.VMEM((16, 2, 128), jnp.float32),
            dma((chunks,)),
            dma((4,)),
            dma((4,)),
            dma((16,)),
            dma((16,)),
            dma((4,)),
            dma((4,)),
            dma((16,)),
            dma((16,)),
            dma((16,)),
            dma((16,)),
        ],
        compiler_params=pltpu.CompilerParams(
            collective_id=0, has_side_effects=True, vmem_limit_bytes=56 << 20
        ),
    )(
        lengths,
        hash_salts,
        acts.reshape(tokens, width_x),
        grads.reshape(tokens, width_g),
        rows,
        domains.reshape(1, domains.shape[0]),
    )
    return grads_out.reshape(ex_dev, 64 * KX), gram


def solution(mesh):
    in_specs = (P("dp", "tok", None), P("dp", "tok", None), P("dp"), P(), P())
    out_specs = (P("dp", "tok"), P())
    return jax.shard_map(body, mesh=mesh, in_specs=in_specs, out_specs=out_specs, check_vma=False)
```

```python
import functools
import math

import jax
import jax.numpy as jnp
import numpy as np
from jax import lax
from jax.experimental import pallas as pl
from jax.experimental.pallas import tpu as pltpu
from jax.sharding import PartitionSpec as P

KX = 256
KG = 256
LEN = 512
DOMAINS = 16
MESH = pl.DeviceIdType.MESH

PR = 46337
INV2 = (PR + 1) // 2
HALF_ROOT = 19963
UNIT = HALF_ROOT * pow(2, 16, PR) % PR
BACK = pow(pow(2, 32, PR), -1, PR)
TURN = (BACK * 2**32 - 1) // PR
STEP_WHOLE = 2**32 // PR
STEP_REST = 2**32 % PR
BIAS = 46343
ROWS = 1024
PAIR = 2 * ROWS


def centered(value):
    value = value % PR
    return value - PR if value > PR // 2 else value


def row_matrix(chunks):
    local = np.arange(ROWS)
    b, a, z = local // 128, local // 8 % 16, local % 8
    out = np.zeros((ROWS, 128), np.float32)
    for offset, digit in ((0, b), (8, b), (16, a), (32, a), (48, z), (56, z)):
        out[local, offset + digit] = 1.0
    for g in range(chunks):
        cross = (ROWS * g + 128 * b) * (8 * a + z) + 8 * a * z
        value = (2 * UNIT * 7919 * 7919 % PR) * (cross % PR) % PR
        value = np.where(value > PR // 2, value - PR, value)
        high = np.round(value / 256)
        out[:, 64 + 2 * g] = high
        out[:, 65 + 2 * g] = value - 256 * high
    return out


def reduced(value):
    return value - float(PR) * jnp.round(value * (1.0 / PR))


def digits(value):
    high = jnp.round(value * (1.0 / 256))
    return high, value - 256.0 * high


def product(left, right):
    high, low = digits(left)
    return reduced(high * reduced(256.0 * right) + low * right)


def iotas(rows):
    row = lax.broadcasted_iota(jnp.int32, (rows, KX), 0).astype(jnp.float32)
    col = lax.broadcasted_iota(jnp.int32, (rows, KX), 1).astype(jnp.float32)
    return row, col


def linear_terms(rows, unit, beta):
    row, _ = iotas(rows)
    slope = reduced(float(centered(2 * UNIT * 7919 * unit)) * row)
    square = reduced(float(centered(UNIT * 7919 * 7919 * unit * unit)) * (row * row))
    line = reduced(float(centered(3 * UNIT * unit)) * row)
    return reduced(product(slope, beta) + square + line)


def column_tables(salt, chunks, first, rall):
    salt = salt.astype(jnp.float32)

    def beta(rows):
        _, col = iotas(rows)
        return reduced(6007.0 * col + salt)

    row, col = iotas(8 * chunks)
    inner = reduced(reduced(float(centered(7919 * 128)) * row) + beta(8 * chunks))
    value = reduced(product(inner, inner) + (384.0 * row + col))
    base_high, base_low = digits(product(jnp.full_like(value, float(centered(UNIT))), value))
    mid_high, mid_low = digits(linear_terms(16, 8, beta(16)))
    low_high, low_low = digits(linear_terms(8, 1, beta(8)))
    pick = lax.broadcasted_iota(jnp.int32, (64, KX), 0)
    for g in range(chunks):
        cross = jnp.where(pick == 2 * g, 256.0, jnp.where(pick == 2 * g + 1, 1.0, 0.0))
        rall[first + g] = jnp.concatenate(
            [
                256.0 * base_high[8 * g : 8 * g + 8],
                base_low[8 * g : 8 * g + 8],
                256.0 * mid_high,
                mid_low,
                256.0 * low_high,
                low_low,
                cross,
            ],
            axis=0,
        ).astype(jnp.bfloat16)


def salt_turn(salt):
    half = jnp.where(salt % 2 == 1, (salt + PR) // 2, salt // 2)
    whole = half * jnp.int32(STEP_WHOLE - 2**32 if STEP_WHOLE >= 2**31 else STEP_WHOLE)
    return whole + (half * STEP_REST) // PR + BIAS


def kernel(
    width_x,
    width_g,
    lengths_ref,
    salts_ref,
    acts_ref,
    grads_ref,
    rows_ref,
    domains_ref,
    eg_ref,
    out_ref,
    xbuf,
    table,
    rall,
    acc,
    px,
    pg_send,
    pg,
    msg,
    dom_slot,
    sum_slot,
    gram_c,
    gram_z,
    in_sem,
    px_ss,
    px_rs,
    pg_ss,
    pg_rs,
    msg_ss,
    msg_rs,
    sum_ss,
    sum_rs,
    gc_ss,
    gc_rs,
    gz_ss,
    gz_rs,
):
    dp, tok = lax.axis_index("dp"), lax.axis_index("tok")
    z, x, yh = lax.div(dp, 8), lax.rem(lax.div(dp, 2), 4), lax.rem(dp, 2)
    yl, core = lax.div(tok, 2), lax.rem(tok, 2)
    y = 2 * yh + yl

    def plane_peer(dz, dyh):
        z_, yh_ = lax.rem(z + dz, 8), lax.rem(yh + dyh, 2)
        return 2 * z_ + yh_, (8 * z_ + 2 * x + yh_, tok)

    def column_peer(dy, dcore):
        y_, core_ = lax.rem(y + dy, 4), lax.rem(core + dcore, 2)
        place = (8 * z + 2 * x + lax.div(y_, 2), 2 * lax.rem(y_, 2) + core_)
        return 2 * y_ + core_, place

    def z_peer(dz):
        z_ = lax.rem(z + dz, 8)
        return z_, (8 * z_ + 2 * x + yh, tok)

    def x_peer(dx):
        x_ = lax.rem(x + dx, 4)
        return x_, (8 * z + 2 * x_ + yh, tok)

    def tok_peer(dyl, dcore):
        to = 2 * lax.rem(yl + dyl, 2) + lax.rem(core + dcore, 2)
        return to, (dp, to)

    ring = (4, 3, 5, 2, 6, 1, 7, 0)
    plane_peers = [plane_peer(dz, d) for dz in ring for d in (1, 0)][:15]
    column_peers = [column_peer(dy, d) for dy in (2, 1, 3, 0) for d in (1, 0)][:7]
    z_peers = [z_peer(dz) for dz in ring[:7]]
    x_peers = [x_peer(dx) for dx in (2, 1, 3)]
    across, diagonal, sibling = tok_peer(1, 0), tok_peer(1, 1), tok_peer(0, 1)

    def remote(source, target, sent, received, device):
        return pltpu.make_async_remote_copy(
            src_ref=source,
            dst_ref=target,
            send_sem=sent,
            recv_sem=received,
            device_id=device,
            device_id_type=MESH,
        )

    def exchange(source, slots, own, peers, sends, receives):
        out, arriving = [], []
        for k, (slot, device) in enumerate(peers):
            here = (source(slot), slots.at[own], sends.at[k], receives.at[own], device)
            there = (source(slot), slots.at[slot], sends.at[k], receives.at[slot], device)
            out.append(functools.partial(remote, *here))
            arriving.append(functools.partial(remote, *there))
        return out, arriving

    n_x, n_g = width_x // PAIR, width_g // PAIR
    n = n_x + n_g
    loads = [
        pltpu.make_async_copy(acts_ref.at[:, pl.ds(c * PAIR, PAIR)], xbuf.at[c], in_sem.at[c])
        for c in range(n_x)
    ] + [
        pltpu.make_async_copy(
            grads_ref.at[:, pl.ds(c * PAIR, PAIR)], xbuf.at[n_x + c], in_sem.at[n_x + c]
        )
        for c in range(n_g)
    ]
    for load in loads:
        load.start()

    barrier = pltpu.get_barrier_semaphore()

    greeted = plane_peers + [p for k, p in enumerate(column_peers) if k != 1] + x_peers
    for _, device in greeted:
        pl.semaphore_signal(barrier, inc=1, device_id=device, device_id_type=MESH)

    salt_x, salt_g = salts_ref[0], salts_ref[1]
    column_tables(salt_x, 2 * n_x, 0, rall)
    column_tables(salt_g, 2 * n_g, 2 * n_x, rall)
    turn_x, turn_g = salt_turn(salt_x), salt_turn(salt_g)
    acc[...] = jnp.zeros_like(acc)

    def make_table(c, slot, turn):
        for half in range(2):
            value = jnp.dot(rows_ref[...], rall[2 * c + half], preferred_element_type=jnp.float32)
            small = (jnp.abs(value) - float(PR)).astype(jnp.int32)
            angle = small * small * jnp.int32(TURN - 2**32) + turn
            sign = jnp.where(angle < 0, 1.0, -1.0).astype(jnp.bfloat16)
            table[slot, pl.ds(half * ROWS, ROWS), :] = sign

    def product_of(c, slot):
        pltpu.make_async_copy(acts_ref.at[:, pl.ds(0, PAIR)], xbuf.at[c], in_sem.at[c]).wait()
        return jnp.dot(xbuf[c], table[slot], preferred_element_type=jnp.float32)

    make_table(0, 0, turn_x)

    def step(c, _):
        slot = lax.rem(c, 2)
        more = product_of(c, slot)
        make_table(c + 1, 1 - slot, turn_x)
        acc[0] += more
        return 0

    lax.fori_loop(0, n_x - 1, step, 0)
    more = product_of(n_x - 1, (n_x - 1) % 2)
    make_table(n_x, n_x % 2, turn_g)
    acc[0] += more

    tokens = acc.shape[1]
    seg = tokens // 2
    position = lax.broadcasted_iota(jnp.int32, (tokens, 1), 0)
    limit = jnp.where(position < seg, lengths_ref[0], lengths_ref[1])
    live = (tok * seg + position % seg < limit).astype(jnp.float32)
    px[tok] = (acc[0] * (live / math.sqrt(width_x))).astype(jnp.bfloat16)
    px_out, px_in = exchange(
        lambda slot: px.at[tok], px, tok, [across, sibling], px_ss, px_rs
    )
    far = across[0]
    forward = functools.partial(
        remote, px.at[far], px.at[far], px_ss.at[2], px_rs.at[far], sibling[1]
    )
    forwarded = functools.partial(
        remote, px.at[far], px.at[diagonal[0]], px_ss.at[2], px_rs.at[diagonal[0]], sibling[1]
    )
    pl.semaphore_wait(barrier, len(greeted))
    for copy in px_out:
        copy().start()

    def step_g(c, _):
        slot = lax.rem(c, 2)
        more = product_of(c, slot)
        make_table(c + 1, 1 - slot, turn_g)
        acc[1] += more
        return 0

    lax.fori_loop(n_x, n - 1, step_g, 0)
    acc[1] += product_of(n - 1, (n - 1) % 2)
    proj_g = (acc[1] * (live / math.sqrt(width_g))).T.astype(jnp.bfloat16)
    for q in range(4):
        pg_send[q] = proj_g[64 * q : 64 * q + 64]
    pg_out, pg_in = exchange(
        lambda slot: pg_send.at[slot], pg, tok, [across, diagonal, sibling], pg_ss, pg_rs
    )
    for copy in pg_out:
        copy().start()
    pg[tok] = pg_send[tok]
    px_in[0]().wait_recv()
    forward().start()

    lane = lax.broadcasted_iota(jnp.int32, (128, 256), 1)
    row = lax.broadcasted_iota(jnp.int32, (128, 256), 0)
    source = lane // 16
    example = 2 * ((source // 2) * 8 + x * 2 + source % 2) + (lane // 8) % 2
    chosen = (row == example).astype(jnp.bfloat16)
    labels = jnp.broadcast_to(domains_ref[...], (8, 128)).astype(jnp.float32).astype(jnp.bfloat16)
    label = jnp.dot(labels, chosen, preferred_element_type=jnp.float32)[0:1].astype(jnp.int32)
    hot = ((label == row % 16) & (row // 16 == lane % 8)).astype(jnp.float32).astype(jnp.bfloat16)

    px_in[1]().wait_recv()
    for copy in pg_in:
        copy().wait_recv()
    forwarded().wait_recv()
    total = []
    for e in range(2):
        left = jnp.concatenate([pg[q, :, e * seg : e * seg + seg] for q in range(4)], axis=1)
        right = jnp.concatenate([px[q, e * seg : e * seg + seg, :] for q in range(4)], axis=0)
        outer = jnp.dot(left, right, preferred_element_type=jnp.float32)
        total.append(outer / math.sqrt(LEN))
    for t in range(16):
        r, c = 8 * (t // 2), 128 * (t % 2)
        msg[t] = jnp.concatenate(
            [total[0][r : r + 8, c : c + 128], total[1][r : r + 8, c : c + 128]], axis=0
        ).astype(jnp.bfloat16)

    here = 2 * z + yh
    msg_out, msg_in = exchange(
        lambda slot: msg.at[slot], dom_slot, here, plane_peers, msg_ss, msg_rs
    )
    for copy in msg_out:
        copy().start()
    dom_slot[here] = msg[here]
    for r in range(64):
        eg_ref[:, KX * r : KX * r + KX] = jnp.concatenate(
            [total[0][r : r + 1], total[1][r : r + 1]], axis=0
        ).astype(jnp.bfloat16)
    for copy in msg_in:
        copy().wait_recv()
    held = dom_slot[...].reshape(256, 128)
    domain_part = jnp.dot(hot, held, preferred_element_type=jnp.float32)

    sum_slot[x] = domain_part.astype(jnp.bfloat16)
    sum_out, sum_in = exchange(lambda slot: sum_slot.at[x], sum_slot, x, x_peers, sum_ss, sum_rs)
    for copy in sum_out:
        copy().start()
    for copy in sum_in:
        copy().wait_recv()
    share = sum(sum_slot[q].astype(jnp.float32) for q in range(4))
    own = jnp.concatenate([share[16 * r : 16 * r + 16] for r in range(8)], axis=1)
    high = own.astype(jnp.bfloat16).astype(jnp.float32)
    low = own - high
    left = jnp.concatenate([high, high, low], axis=1).astype(jnp.bfloat16)
    right = jnp.concatenate([high, low, high], axis=1)
    right = jnp.concatenate([right] * 8, axis=0).astype(jnp.bfloat16)
    wide = lax.dot_general(
        left, right, (((1,), (1,)), ((), ())), preferred_element_type=jnp.float32
    )
    on_diagonal = (
        lax.broadcasted_iota(jnp.int32, (16, 128), 1) // 16
        == lax.broadcasted_iota(jnp.int32, (16, 128), 0) % 8
    )
    wide = jnp.where(on_diagonal, wide, 0.0)
    flat = jnp.concatenate(
        [jnp.sum(wide[:8], axis=0, keepdims=True), jnp.sum(wide[8:], axis=0, keepdims=True)], axis=0
    )

    pending = px_out + [forward] + pg_out + msg_out + sum_out
    for slots, own_slot, peers, sends, receives in (
        (gram_c, 2 * y + core, column_peers, gc_ss, gc_rs),
        (gram_z, z, z_peers, gz_ss, gz_rs),
    ):
        slots[own_slot] = flat
        gram_out, gram_in = exchange(
            lambda slot: slots.at[own_slot], slots, own_slot, peers, sends, receives
        )
        for copy in gram_out:
            copy().start()
        for copy in pending:
            copy().wait_send()
        pending = gram_out
        for copy in gram_in:
            copy().wait_recv()
        flat = jnp.sum(slots[...], axis=0)
    for copy in pending:
        copy().wait_send()
    spread = jnp.concatenate(
        [jnp.broadcast_to(flat[0:1], (8, 128)), jnp.broadcast_to(flat[1:2], (8, 128))], axis=0
    )
    spread = jnp.where(on_diagonal, spread, 0.0)
    fold = (
        lax.broadcasted_iota(jnp.int32, (128, 16), 0) % 16
        == lax.broadcasted_iota(jnp.int32, (128, 16), 1)
    ).astype(jnp.float32)
    out_ref[...] = jnp.dot(
        spread, fold, precision=lax.Precision.HIGHEST, preferred_element_type=jnp.float32
    ) / (16.0 * KX * KG)


def keep(eg_ref, gram_ref, eg_out, gram_out):
    eg_out[...] = eg_ref[...]
    gram_out[...] = gram_ref[...]


def body(acts, grads, lengths, domains, hash_salts):
    ex_dev, seg, width_x = acts.shape
    width_g = grads.shape[2]
    tokens = ex_dev * seg
    chunks = (width_x + width_g) // PAIR
    rows = jnp.asarray(row_matrix(width_x // ROWS), jnp.bfloat16)
    dma = pltpu.SemaphoreType.DMA
    vmem = pl.BlockSpec(memory_space=pltpu.VMEM)
    results = (
        jax.ShapeDtypeStruct((ex_dev, 64 * KX), jnp.bfloat16),
        jax.ShapeDtypeStruct((DOMAINS, DOMAINS), jnp.float32),
    )
    made = pl.pallas_call(
        functools.partial(kernel, width_x, width_g),
        out_shape=results,
        in_specs=[
            pl.BlockSpec(memory_space=pltpu.SMEM),
            pl.BlockSpec(memory_space=pltpu.SMEM),
            pl.BlockSpec(memory_space=pl.ANY),
            pl.BlockSpec(memory_space=pl.ANY),
            vmem,
            vmem,
        ],
        out_specs=(vmem, vmem),
        scratch_shapes=[
            pltpu.VMEM((chunks, tokens, PAIR), jnp.bfloat16),
            pltpu.VMEM((2, PAIR, KX), jnp.bfloat16),
            pltpu.VMEM((2 * chunks, 128, KX), jnp.bfloat16),
            pltpu.VMEM((2, tokens, KX), jnp.float32),
            pltpu.VMEM((4, tokens, KX), jnp.bfloat16),
            pltpu.VMEM((4, 64, tokens), jnp.bfloat16),
            pltpu.VMEM((4, 64, tokens), jnp.bfloat16),
            pltpu.VMEM((16, 16, 128), jnp.bfloat16),
            pltpu.VMEM((16, 16, 128), jnp.bfloat16),
            pltpu.VMEM((4, 128, 128), jnp.bfloat16),
            pltpu.VMEM((8, 2, 128), jnp.float32),
            pltpu.VMEM((8, 2, 128), jnp.float32),
            dma((chunks,)),
            dma((4,)),
            dma((4,)),
            dma((4,)),
            dma((4,)),
            dma((16,)),
            dma((16,)),
            dma((4,)),
            dma((4,)),
            dma((8,)),
            dma((8,)),
            dma((8,)),
            dma((8,)),
        ],
        compiler_params=pltpu.CompilerParams(
            collective_id=0, has_side_effects=True, vmem_limit_bytes=56 << 20
        ),
    )(
        lengths,
        hash_salts,
        acts.reshape(tokens, width_x),
        grads.reshape(tokens, width_g),
        rows,
        domains.reshape(1, domains.shape[0]),
    )
    return pl.pallas_call(keep, out_shape=results, in_specs=[vmem] * 2, out_specs=(vmem, vmem))(*made)


def solution(mesh):
    in_specs = (P("dp", "tok", None), P("dp", "tok", None), P("dp"), P(), P())
    out_specs = (P("dp", "tok"), P())
    return jax.shard_map(body, mesh=mesh, in_specs=in_specs, out_specs=out_specs, check_vma=False)
```

```python
import functools
import math

import jax
import jax.numpy as jnp
import numpy as np
from jax import lax
from jax.experimental import pallas as pl
from jax.experimental.pallas import tpu as pltpu
from jax.sharding import PartitionSpec as P

KX = 256
KG = 256
LEN = 512
DOMAINS = 16
MESH = pl.DeviceIdType.MESH

PR = 46337
INV2 = (PR + 1) // 2
HALF_ROOT = 19963
UNIT = HALF_ROOT * pow(2, 16, PR) % PR
BACK = pow(pow(2, 32, PR), -1, PR)
TURN = (BACK * 2**32 - 1) // PR
STEP_WHOLE = 2**32 // PR
STEP_REST = 2**32 % PR
BIAS = 46343
ROWS = 1024
PAIR = 2 * ROWS


def centered(value):
    value = value % PR
    return value - PR if value > PR // 2 else value


def row_matrix(chunks):
    local = np.arange(ROWS)
    b, a, z = local // 128, local // 8 % 16, local % 8
    out = np.zeros((ROWS, 128), np.float32)
    for offset, digit in ((0, b), (8, b), (16, a), (32, a), (48, z), (56, z)):
        out[local, offset + digit] = 1.0
    for g in range(chunks):
        cross = (ROWS * g + 128 * b) * (8 * a + z) + 8 * a * z
        value = (2 * UNIT * 7919 * 7919 % PR) * (cross % PR) % PR
        value = np.where(value > PR // 2, value - PR, value)
        high = np.round(value / 256)
        out[:, 64 + 2 * g] = high
        out[:, 65 + 2 * g] = value - 256 * high
    return out


def reduced(value):
    return value - float(PR) * jnp.round(value * (1.0 / PR))


def digits(value):
    high = jnp.round(value * (1.0 / 256))
    return high, value - 256.0 * high


def product(left, right):
    high, low = digits(left)
    return reduced(high * reduced(256.0 * right) + low * right)


def iotas(rows):
    row = lax.broadcasted_iota(jnp.int32, (rows, KX), 0).astype(jnp.float32)
    col = lax.broadcasted_iota(jnp.int32, (rows, KX), 1).astype(jnp.float32)
    return row, col


def linear_terms(rows, unit, beta):
    row, _ = iotas(rows)
    slope = reduced(float(centered(2 * UNIT * 7919 * unit)) * row)
    square = reduced(float(centered(UNIT * 7919 * 7919 * unit * unit)) * (row * row))
    line = reduced(float(centered(3 * UNIT * unit)) * row)
    return reduced(product(slope, beta) + square + line)


def column_tables(salt, chunks, first, rall):
    salt = salt.astype(jnp.float32)

    def beta(rows):
        _, col = iotas(rows)
        return reduced(6007.0 * col + salt)

    row, col = iotas(8 * chunks)
    inner = reduced(reduced(float(centered(7919 * 128)) * row) + beta(8 * chunks))
    value = reduced(product(inner, inner) + (384.0 * row + col))
    base_high, base_low = digits(product(jnp.full_like(value, float(centered(UNIT))), value))
    mid_high, mid_low = digits(linear_terms(16, 8, beta(16)))
    low_high, low_low = digits(linear_terms(8, 1, beta(8)))
    pick = lax.broadcasted_iota(jnp.int32, (64, KX), 0)
    for g in range(chunks):
        cross = jnp.where(pick == 2 * g, 256.0, jnp.where(pick == 2 * g + 1, 1.0, 0.0))
        rall[first + g] = jnp.concatenate(
            [
                256.0 * base_high[8 * g : 8 * g + 8],
                base_low[8 * g : 8 * g + 8],
                256.0 * mid_high,
                mid_low,
                256.0 * low_high,
                low_low,
                cross,
            ],
            axis=0,
        ).astype(jnp.bfloat16)


def salt_turn(salt):
    half = jnp.where(salt % 2 == 1, (salt + PR) // 2, salt // 2)
    whole = half * jnp.int32(STEP_WHOLE - 2**32 if STEP_WHOLE >= 2**31 else STEP_WHOLE)
    return whole + (half * STEP_REST) // PR + BIAS


def kernel(
    width_x,
    width_g,
    lengths_ref,
    salts_ref,
    acts_ref,
    grads_ref,
    rows_ref,
    domains_ref,
    eg_ref,
    out_ref,
    xbuf,
    table,
    rall,
    acc,
    px,
    pg_send,
    pg,
    msg,
    dom_slot,
    sum_slot,
    gram_c,
    gram_z,
    in_sem,
    px_ss,
    px_rs,
    pg_ss,
    pg_rs,
    msg_ss,
    msg_rs,
    sum_ss,
    sum_rs,
    gc_ss,
    gc_rs,
    gz_ss,
    gz_rs,
):
    dp, tok = lax.axis_index("dp"), lax.axis_index("tok")
    z, x, yh = lax.div(dp, 8), lax.rem(lax.div(dp, 2), 4), lax.rem(dp, 2)
    yl, core = lax.div(tok, 2), lax.rem(tok, 2)
    y = 2 * yh + yl

    def plane_peer(dz, dyh):
        z_, yh_ = lax.rem(z + dz, 8), lax.rem(yh + dyh, 2)
        return 2 * z_ + yh_, (8 * z_ + 2 * x + yh_, tok)

    def column_peer(dy, dcore):
        y_, core_ = lax.rem(y + dy, 4), lax.rem(core + dcore, 2)
        place = (8 * z + 2 * x + lax.div(y_, 2), 2 * lax.rem(y_, 2) + core_)
        return 2 * y_ + core_, place

    def z_peer(dz):
        z_ = lax.rem(z + dz, 8)
        return z_, (8 * z_ + 2 * x + yh, tok)

    def x_peer(dx):
        x_ = lax.rem(x + dx, 4)
        return x_, (8 * z + 2 * x_ + yh, tok)

    def tok_peer(dyl, dcore):
        to = 2 * lax.rem(yl + dyl, 2) + lax.rem(core + dcore, 2)
        return to, (dp, to)

    ring = (4, 3, 5, 2, 6, 1, 7, 0)
    plane_peers = [plane_peer(dz, d) for dz in ring for d in (1, 0)][:15]
    column_peers = [column_peer(dy, d) for dy in (2, 1, 3, 0) for d in (1, 0)][:7]
    z_peers = [z_peer(dz) for dz in ring[:7]]
    x_peers = [x_peer(dx) for dx in (2, 1, 3)]
    across, diagonal, sibling = tok_peer(1, 0), tok_peer(1, 1), tok_peer(0, 1)

    def remote(source, target, sent, received, device):
        return pltpu.make_async_remote_copy(
            src_ref=source,
            dst_ref=target,
            send_sem=sent,
            recv_sem=received,
            device_id=device,
            device_id_type=MESH,
        )

    def exchange(source, slots, own, peers, sends, receives):
        out, arriving = [], []
        for k, (slot, device) in enumerate(peers):
            here = (source(slot), slots.at[own], sends.at[k], receives.at[own], device)
            there = (source(slot), slots.at[slot], sends.at[k], receives.at[slot], device)
            out.append(functools.partial(remote, *here))
            arriving.append(functools.partial(remote, *there))
        return out, arriving

    n_x, n_g = width_x // PAIR, width_g // PAIR
    n = n_x + n_g
    loads = [
        pltpu.make_async_copy(acts_ref.at[:, pl.ds(c * PAIR, PAIR)], xbuf.at[c], in_sem.at[c])
        for c in range(n_x)
    ] + [
        pltpu.make_async_copy(
            grads_ref.at[:, pl.ds(c * PAIR, PAIR)], xbuf.at[n_x + c], in_sem.at[n_x + c]
        )
        for c in range(n_g)
    ]
    for load in loads:
        load.start()

    barrier = pltpu.get_barrier_semaphore()

    greeted = plane_peers + [p for k, p in enumerate(column_peers) if k != 1] + x_peers
    for _, device in greeted:
        pl.semaphore_signal(barrier, inc=1, device_id=device, device_id_type=MESH)

    salt_x, salt_g = salts_ref[0], salts_ref[1]
    column_tables(salt_x, 2 * n_x, 0, rall)
    column_tables(salt_g, 2 * n_g, 2 * n_x, rall)
    turn_x, turn_g = salt_turn(salt_x), salt_turn(salt_g)
    acc[...] = jnp.zeros_like(acc)

    def make_table(c, slot, turn):
        for half in range(2):
            value = jnp.dot(rows_ref[...], rall[2 * c + half], preferred_element_type=jnp.float32)
            small = (jnp.abs(value) - float(PR)).astype(jnp.int32)
            angle = small * small * jnp.int32(TURN - 2**32) + turn
            sign = jnp.where(angle < 0, 1.0, -1.0).astype(jnp.bfloat16)
            table[slot, pl.ds(half * ROWS, ROWS), :] = sign

    waits = {0: range(2), 2: range(2, 5), 5: range(5, n)}

    def product_of(c, slot):
        for arrived in waits.get(c, ()):
            loads[arrived].wait()
        return jnp.dot(xbuf[c], table[slot], preferred_element_type=jnp.float32)

    make_table(0, 0, turn_x)

    for c in range(n_x - 1):
        slot = c % 2
        more = product_of(c, slot)
        make_table(c + 1, 1 - slot, turn_x)
        acc[0] += more

    more = product_of(n_x - 1, (n_x - 1) % 2)
    make_table(n_x, n_x % 2, turn_g)
    acc[0] += more

    tokens = acc.shape[1]
    seg = tokens // 2
    position = lax.broadcasted_iota(jnp.int32, (tokens, 1), 0)
    limit = jnp.where(position < seg, lengths_ref[0], lengths_ref[1])
    live = (tok * seg + position % seg < limit).astype(jnp.float32)
    scaled = (acc[0] * (live / math.sqrt(width_x))).astype(jnp.bfloat16)
    px[tok, 0] = scaled[:seg]
    px[tok, 1] = scaled[seg:]
    far, near, other = across[0], sibling[0], diagonal[0]

    def px_copy(source, slot, half, sent, device):
        there = px.at[slot, half]
        return remote(px.at[source, half], there, px_ss.at[sent + half], px_rs.at[slot, half], device)

    px_out = [functools.partial(px_copy, tok, tok, half, 0, across[1]) for half in range(2)]
    px_out += [functools.partial(px_copy, tok, tok, half, 2, sibling[1]) for half in range(2)]
    forward = [functools.partial(px_copy, far, far, half, 4, sibling[1]) for half in range(2)]
    px_far = [functools.partial(px_copy, tok, far, half, 0, across[1]) for half in range(2)]
    px_near = [functools.partial(px_copy, tok, near, half, 2, sibling[1]) for half in range(2)]
    px_other = [functools.partial(px_copy, far, other, half, 4, sibling[1]) for half in range(2)]
    pl.semaphore_wait(barrier, len(greeted))
    for copy in px_out:
        copy().start()

    for c in range(n_x, n - 1):
        slot = c % 2
        more = product_of(c, slot)
        make_table(c + 1, 1 - slot, turn_g)
        acc[1] += more

    acc[1] += product_of(n - 1, (n - 1) % 2)
    proj_g = (acc[1] * (live / math.sqrt(width_g))).T.astype(jnp.bfloat16)
    for q in range(4):
        pg_send[q] = proj_g[64 * q : 64 * q + 64]
    pg_out, pg_in = exchange(
        lambda slot: pg_send.at[slot], pg, tok, [across, diagonal, sibling], pg_ss, pg_rs
    )
    for copy in pg_out:
        copy().start()
    pg[tok] = pg_send[tok]
    for half in range(2):
        px_far[half]().wait_recv()
        forward[half]().start()

    lane = lax.broadcasted_iota(jnp.int32, (128, 256), 1)
    row = lax.broadcasted_iota(jnp.int32, (128, 256), 0)
    source = lane // 16
    example = 2 * ((source // 2) * 8 + x * 2 + source % 2) + (lane // 8) % 2
    chosen = (row == example).astype(jnp.bfloat16)
    labels = jnp.broadcast_to(domains_ref[...], (8, 128)).astype(jnp.float32).astype(jnp.bfloat16)
    label = jnp.dot(labels, chosen, preferred_element_type=jnp.float32)[0:1].astype(jnp.int32)
    hot = ((label == row % 16) & (row // 16 == lane % 8)).astype(jnp.float32).astype(jnp.bfloat16)

    for copy in px_near + pg_in + px_other:
        copy().wait_recv()
    total = []
    for e in range(2):
        left = jnp.concatenate([pg[q, :, e * seg : e * seg + seg] for q in range(4)], axis=1)
        right = jnp.concatenate([px[q, e] for q in range(4)], axis=0)
        outer = jnp.dot(left, right, preferred_element_type=jnp.float32)
        total.append(outer * (1.0 / math.sqrt(LEN)))
    for t in range(16):
        r, c = 8 * (t // 2), 128 * (t % 2)
        msg[t] = jnp.concatenate(
            [total[0][r : r + 8, c : c + 128], total[1][r : r + 8, c : c + 128]], axis=0
        ).astype(jnp.bfloat16)

    here = 2 * z + yh
    msg_out, msg_in = exchange(
        lambda slot: msg.at[slot], dom_slot, here, plane_peers, msg_ss, msg_rs
    )
    for copy in msg_out:
        copy().start()
    dom_slot[here] = msg[here]
    for r in range(64):
        eg_ref[:, KX * r : KX * r + KX] = jnp.concatenate(
            [total[0][r : r + 1], total[1][r : r + 1]], axis=0
        ).astype(jnp.bfloat16)
    for copy in msg_in:
        copy().wait_recv()
    held = dom_slot[...].reshape(256, 128)
    domain_part = jnp.dot(hot, held, preferred_element_type=jnp.float32)

    sum_slot[x] = domain_part.astype(jnp.bfloat16)
    sum_out, sum_in = exchange(lambda slot: sum_slot.at[x], sum_slot, x, x_peers, sum_ss, sum_rs)
    for copy in sum_out:
        copy().start()
    for copy in sum_in:
        copy().wait_recv()
    share = sum(sum_slot[q].astype(jnp.float32) for q in range(4))
    own = jnp.concatenate([share[16 * r : 16 * r + 16] for r in range(8)], axis=1)
    high = own.astype(jnp.bfloat16).astype(jnp.float32)
    low = own - high
    left = jnp.concatenate([high, high, low], axis=1).astype(jnp.bfloat16)
    right = jnp.concatenate([high, low, high], axis=1)
    right = jnp.concatenate([right] * 8, axis=0).astype(jnp.bfloat16)
    wide = lax.dot_general(
        left, right, (((1,), (1,)), ((), ())), preferred_element_type=jnp.float32
    )
    on_diagonal = (
        lax.broadcasted_iota(jnp.int32, (16, 128), 1) // 16
        == lax.broadcasted_iota(jnp.int32, (16, 128), 0) % 8
    )
    wide = jnp.where(on_diagonal, wide, 0.0)
    flat = jnp.concatenate(
        [jnp.sum(wide[:8], axis=0, keepdims=True), jnp.sum(wide[8:], axis=0, keepdims=True)], axis=0
    )

    pending = px_out + forward + pg_out + msg_out + sum_out
    for slots, own_slot, peers, sends, receives in (
        (gram_c, 2 * y + core, column_peers, gc_ss, gc_rs),
        (gram_z, z, z_peers, gz_ss, gz_rs),
    ):
        slots[own_slot] = flat
        gram_out, gram_in = exchange(
            lambda slot: slots.at[own_slot], slots, own_slot, peers, sends, receives
        )
        for copy in gram_out:
            copy().start()
        for copy in pending:
            copy().wait_send()
        pending = gram_out
        for copy in gram_in:
            copy().wait_recv()
        flat = jnp.sum(slots[...], axis=0)
    for copy in pending:
        copy().wait_send()
    spread = jnp.concatenate(
        [jnp.broadcast_to(flat[0:1], (8, 128)), jnp.broadcast_to(flat[1:2], (8, 128))], axis=0
    )
    spread = jnp.where(on_diagonal, spread, 0.0)
    fold = (
        lax.broadcasted_iota(jnp.int32, (384, 16), 0) % 16
        == lax.broadcasted_iota(jnp.int32, (384, 16), 1)
    ).astype(jnp.bfloat16)
    high = spread.astype(jnp.bfloat16).astype(jnp.float32)
    middle = (spread - high).astype(jnp.bfloat16).astype(jnp.float32)
    pieces = jnp.concatenate([high, middle, spread - high - middle], axis=1).astype(jnp.bfloat16)
    out_ref[...] = jnp.dot(pieces, fold, preferred_element_type=jnp.float32) / (16.0 * KX * KG)


def keep(eg_ref, gram_ref, eg_out, gram_out):
    eg_out[...] = eg_ref[...]
    gram_out[...] = gram_ref[...]


def body(acts, grads, lengths, domains, hash_salts):
    ex_dev, seg, width_x = acts.shape
    width_g = grads.shape[2]
    tokens = ex_dev * seg
    chunks = (width_x + width_g) // PAIR
    rows = jnp.asarray(row_matrix(width_x // ROWS), jnp.bfloat16)
    dma = pltpu.SemaphoreType.DMA
    vmem = pl.BlockSpec(memory_space=pltpu.VMEM)
    results = (
        jax.ShapeDtypeStruct((ex_dev, 64 * KX), jnp.bfloat16),
        jax.ShapeDtypeStruct((DOMAINS, DOMAINS), jnp.float32),
    )
    made = pl.pallas_call(
        functools.partial(kernel, width_x, width_g),
        out_shape=results,
        in_specs=[
            pl.BlockSpec(memory_space=pltpu.SMEM),
            pl.BlockSpec(memory_space=pltpu.SMEM),
            pl.BlockSpec(memory_space=pl.ANY),
            pl.BlockSpec(memory_space=pl.ANY),
            vmem,
            vmem,
        ],
        out_specs=(vmem, vmem),
        scratch_shapes=[
            pltpu.VMEM((chunks, tokens, PAIR), jnp.bfloat16),
            pltpu.VMEM((2, PAIR, KX), jnp.bfloat16),
            pltpu.VMEM((2 * chunks, 128, KX), jnp.bfloat16),
            pltpu.VMEM((2, tokens, KX), jnp.float32),
            pltpu.VMEM((4, ex_dev, seg, KX), jnp.bfloat16),
            pltpu.VMEM((4, 64, tokens), jnp.bfloat16),
            pltpu.VMEM((4, 64, tokens), jnp.bfloat16),
            pltpu.VMEM((16, 16, 128), jnp.bfloat16),
            pltpu.VMEM((16, 16, 128), jnp.bfloat16),
            pltpu.VMEM((4, 128, 128), jnp.bfloat16),
            pltpu.VMEM((8, 2, 128), jnp.float32),
            pltpu.VMEM((8, 2, 128), jnp.float32),
            dma((chunks,)),
            dma((6,)),
            dma((4, 2)),
            dma((4,)),
            dma((4,)),
            dma((16,)),
            dma((16,)),
            dma((4,)),
            dma((4,)),
            dma((8,)),
            dma((8,)),
            dma((8,)),
            dma((8,)),
        ],
        compiler_params=pltpu.CompilerParams(
            collective_id=0, has_side_effects=True, vmem_limit_bytes=56 << 20
        ),
    )(
        lengths,
        hash_salts,
        acts.reshape(tokens, width_x),
        grads.reshape(tokens, width_g),
        rows,
        domains.reshape(1, domains.shape[0]),
    )
    return pl.pallas_call(keep, out_shape=results, in_specs=[vmem] * 2, out_specs=(vmem, vmem))(*made)


def solution(mesh):
    in_specs = (P("dp", "tok", None), P("dp", "tok", None), P("dp"), P(), P())
    out_specs = (P("dp", "tok"), P())
    return jax.shard_map(body, mesh=mesh, in_specs=in_specs, out_specs=out_specs, check_vma=False)
```

```python
import functools
import math

import jax
import jax.numpy as jnp
import numpy as np
from jax import lax
from jax.experimental import pallas as pl
from jax.experimental.pallas import tpu as pltpu
from jax.sharding import PartitionSpec as P

KX = 256
KG = 256
LEN = 512
DOMAINS = 16
MESH = pl.DeviceIdType.MESH

PR = 46337
INV2 = (PR + 1) // 2
HALF_ROOT = 19963
UNIT = HALF_ROOT * pow(2, 16, PR) % PR
BACK = pow(pow(2, 32, PR), -1, PR)
TURN = (BACK * 2**32 - 1) // PR
STEP_WHOLE = 2**32 // PR
STEP_REST = 2**32 % PR
BIAS = 46343
ROWS = 1024
PAIR = 2 * ROWS


def centered(value):
    value = value % PR
    return value - PR if value > PR // 2 else value


def row_matrix(chunks):
    local = np.arange(ROWS)
    b, a, z = local // 128, local // 8 % 16, local % 8
    out = np.zeros((ROWS, 128), np.float32)
    for offset, digit in ((0, b), (8, b), (16, a), (32, a), (48, z), (56, z)):
        out[local, offset + digit] = 1.0
    for g in range(chunks):
        cross = (ROWS * g + 128 * b) * (8 * a + z) + 8 * a * z
        value = (2 * UNIT * 7919 * 7919 % PR) * (cross % PR) % PR
        value = np.where(value > PR // 2, value - PR, value)
        high = np.round(value / 256)
        out[:, 64 + 2 * g] = high
        out[:, 65 + 2 * g] = value - 256 * high
    return out


def reduced(value):
    return value - float(PR) * jnp.round(value * (1.0 / PR))


def digits(value):
    high = jnp.round(value * (1.0 / 256))
    return high, value - 256.0 * high


def product(left, right):
    high, low = digits(left)
    return reduced(high * reduced(256.0 * right) + low * right)


def iotas(rows):
    row = lax.broadcasted_iota(jnp.int32, (rows, KX), 0).astype(jnp.float32)
    col = lax.broadcasted_iota(jnp.int32, (rows, KX), 1).astype(jnp.float32)
    return row, col


def linear_terms(rows, unit, beta):
    row, _ = iotas(rows)
    slope = reduced(float(centered(2 * UNIT * 7919 * unit)) * row)
    square = reduced(float(centered(UNIT * 7919 * 7919 * unit * unit)) * (row * row))
    line = reduced(float(centered(3 * UNIT * unit)) * row)
    return reduced(product(slope, beta) + square + line)


def column_tables(salt, chunks, first, rall):
    salt = salt.astype(jnp.float32)

    def beta(rows):
        _, col = iotas(rows)
        return reduced(6007.0 * col + salt)

    row, col = iotas(8 * chunks)
    inner = reduced(reduced(float(centered(7919 * 128)) * row) + beta(8 * chunks))
    value = reduced(product(inner, inner) + (384.0 * row + col))
    base_high, base_low = digits(product(jnp.full_like(value, float(centered(UNIT))), value))
    mid_high, mid_low = digits(linear_terms(16, 8, beta(16)))
    low_high, low_low = digits(linear_terms(8, 1, beta(8)))
    pick = lax.broadcasted_iota(jnp.int32, (64, KX), 0)
    for g in range(chunks):
        cross = jnp.where(pick == 2 * g, 256.0, jnp.where(pick == 2 * g + 1, 1.0, 0.0))
        rall[first + g] = jnp.concatenate(
            [
                256.0 * base_high[8 * g : 8 * g + 8],
                base_low[8 * g : 8 * g + 8],
                256.0 * mid_high,
                mid_low,
                256.0 * low_high,
                low_low,
                cross,
            ],
            axis=0,
        ).astype(jnp.bfloat16)


def salt_turn(salt):
    half = jnp.where(salt % 2 == 1, (salt + PR) // 2, salt // 2)
    whole = half * jnp.int32(STEP_WHOLE - 2**32 if STEP_WHOLE >= 2**31 else STEP_WHOLE)
    return whole + (half * STEP_REST) // PR + BIAS


def kernel(
    width_x,
    width_g,
    lengths_ref,
    salts_ref,
    acts_ref,
    grads_ref,
    rows_ref,
    domains_ref,
    eg_ref,
    out_ref,
    xbuf,
    table,
    rall,
    acc,
    px,
    pg_send,
    pg,
    msg,
    dom_slot,
    sum_slot,
    gram_c,
    gram_z,
    in_sem,
    px_ss,
    px_rs,
    pg_ss,
    pg_rs,
    msg_ss,
    msg_rs,
    sum_ss,
    sum_rs,
    gc_ss,
    gc_rs,
    gz_ss,
    gz_rs,
):
    dp, tok = lax.axis_index("dp"), lax.axis_index("tok")
    z, x, yh = lax.div(dp, 8), lax.rem(lax.div(dp, 2), 4), lax.rem(dp, 2)
    yl, core = lax.div(tok, 2), lax.rem(tok, 2)
    y = 2 * yh + yl

    def plane_peer(dz, dyh):
        z_, yh_ = lax.rem(z + dz, 8), lax.rem(yh + dyh, 2)
        return 2 * z_ + yh_, (8 * z_ + 2 * x + yh_, tok)

    def column_peer(dy, dcore):
        y_, core_ = lax.rem(y + dy, 4), lax.rem(core + dcore, 2)
        place = (8 * z + 2 * x + lax.div(y_, 2), 2 * lax.rem(y_, 2) + core_)
        return 2 * y_ + core_, place

    def z_peer(dz):
        z_ = lax.rem(z + dz, 8)
        return z_, (8 * z_ + 2 * x + yh, tok)

    def x_peer(dx):
        x_ = lax.rem(x + dx, 4)
        return x_, (8 * z + 2 * x_ + yh, tok)

    def tok_peer(dyl, dcore):
        to = 2 * lax.rem(yl + dyl, 2) + lax.rem(core + dcore, 2)
        return to, (dp, to)

    ring = (4, 3, 5, 2, 6, 1, 7, 0)
    plane_peers = [plane_peer(dz, d) for dz in ring for d in (1, 0)][:15]
    column_peers = [column_peer(dy, d) for dy in (2, 1, 3, 0) for d in (1, 0)][:7]
    z_peers = [z_peer(dz) for dz in ring[:7]]
    x_peers = [x_peer(dx) for dx in (2, 1, 3)]
    across, diagonal, sibling = tok_peer(1, 0), tok_peer(1, 1), tok_peer(0, 1)

    def remote(source, target, sent, received, device):
        return pltpu.make_async_remote_copy(
            src_ref=source,
            dst_ref=target,
            send_sem=sent,
            recv_sem=received,
            device_id=device,
            device_id_type=MESH,
        )

    def exchange(source, slots, own, peers, sends, receives):
        out, arriving = [], []
        for k, (slot, device) in enumerate(peers):
            here = (source(slot), slots.at[own], sends.at[k], receives.at[own], device)
            there = (source(slot), slots.at[slot], sends.at[k], receives.at[slot], device)
            out.append(functools.partial(remote, *here))
            arriving.append(functools.partial(remote, *there))
        return out, arriving

    n_x, n_g = width_x // PAIR, width_g // PAIR
    n = n_x + n_g
    loads = [
        pltpu.make_async_copy(acts_ref.at[:, pl.ds(c * PAIR, PAIR)], xbuf.at[c], in_sem.at[c])
        for c in range(n_x)
    ] + [
        pltpu.make_async_copy(
            grads_ref.at[:, pl.ds(c * PAIR, PAIR)], xbuf.at[n_x + c], in_sem.at[n_x + c]
        )
        for c in range(n_g)
    ]
    for load in loads:
        load.start()

    barrier = pltpu.get_barrier_semaphore()

    greeted = plane_peers + [p for k, p in enumerate(column_peers) if k != 1] + x_peers
    for _, device in greeted:
        pl.semaphore_signal(barrier, inc=1, device_id=device, device_id_type=MESH)

    salt_x, salt_g = salts_ref[0], salts_ref[1]
    column_tables(salt_x, 2 * n_x, 0, rall)
    column_tables(salt_g, 2 * n_g, 2 * n_x, rall)
    turn_x, turn_g = salt_turn(salt_x), salt_turn(salt_g)

    def make_table(c, slot, turn):
        for half in range(2):
            value = jnp.dot(rows_ref[...], rall[2 * c + half], preferred_element_type=jnp.float32)
            small = (jnp.abs(value) - float(PR)).astype(jnp.int32)
            angle = small * small * jnp.int32(TURN - 2**32) + turn
            sign = jnp.where(angle < 0, 1.0, -1.0).astype(jnp.bfloat16)
            table[slot, pl.ds(half * ROWS, ROWS), :] = sign

    waits = {0: range(2), 2: range(2, 5), 5: range(5, n)}

    def product_of(c, slot):
        for arrived in waits.get(c, ()):
            loads[arrived].wait()
        return jnp.dot(xbuf[c], table[slot], preferred_element_type=jnp.float32)

    make_table(0, 0, turn_x)

    for c in range(n_x - 1):
        slot = c % 2
        more = product_of(c, slot)
        make_table(c + 1, 1 - slot, turn_x)
        acc[0] = more if c == 0 else acc[0] + more

    more = product_of(n_x - 1, (n_x - 1) % 2)
    make_table(n_x, n_x % 2, turn_g)
    acc[0] += more

    tokens = acc.shape[1]
    seg = tokens // 2
    position = lax.broadcasted_iota(jnp.int32, (tokens, 1), 0)
    limit = jnp.where(position < seg, lengths_ref[0], lengths_ref[1])
    live = (tok * seg + position % seg < limit).astype(jnp.float32)
    scaled = (acc[0] * (live / math.sqrt(width_x))).astype(jnp.bfloat16)
    px[tok, 0] = scaled[:seg]
    px[tok, 1] = scaled[seg:]
    far, near, other = across[0], sibling[0], diagonal[0]

    def px_copy(source, slot, half, sent, device):
        there = px.at[slot, half]
        return remote(px.at[source, half], there, px_ss.at[sent + half], px_rs.at[slot, half], device)

    px_out = [functools.partial(px_copy, tok, tok, half, 0, across[1]) for half in range(2)]
    px_out += [functools.partial(px_copy, tok, tok, half, 2, sibling[1]) for half in range(2)]
    forward = [functools.partial(px_copy, far, far, half, 4, sibling[1]) for half in range(2)]
    px_far = [functools.partial(px_copy, tok, far, half, 0, across[1]) for half in range(2)]
    px_near = [functools.partial(px_copy, tok, near, half, 2, sibling[1]) for half in range(2)]
    px_other = [functools.partial(px_copy, far, other, half, 4, sibling[1]) for half in range(2)]
    pl.semaphore_wait(barrier, len(greeted))
    for copy in px_out:
        copy().start()

    for c in range(n_x, n - 1):
        slot = c % 2
        more = product_of(c, slot)
        make_table(c + 1, 1 - slot, turn_g)
        acc[1] = more if c == n_x else acc[1] + more

    acc[1] += product_of(n - 1, (n - 1) % 2)
    proj_g = (acc[1] * (live / math.sqrt(width_g))).T.astype(jnp.bfloat16)
    for q in range(4):
        pg_send[q] = proj_g[64 * q : 64 * q + 64]
    pg_out, pg_in = exchange(
        lambda slot: pg_send.at[slot], pg, tok, [across, diagonal, sibling], pg_ss, pg_rs
    )
    for copy in pg_out:
        copy().start()
    pg[tok] = pg_send[tok]
    for half in range(2):
        px_far[half]().wait_recv()
        forward[half]().start()

    lane = lax.broadcasted_iota(jnp.int32, (128, 256), 1)
    row = lax.broadcasted_iota(jnp.int32, (128, 256), 0)
    source = lane // 16
    example = 2 * ((source // 2) * 8 + x * 2 + source % 2) + (lane // 8) % 2
    chosen = (row == example).astype(jnp.bfloat16)
    labels = jnp.broadcast_to(domains_ref[...], (8, 128)).astype(jnp.float32).astype(jnp.bfloat16)
    label = jnp.dot(labels, chosen, preferred_element_type=jnp.float32)[0:1].astype(jnp.int32)
    hot = ((label == row % 16) & (row // 16 == lane % 8)).astype(jnp.float32).astype(jnp.bfloat16)

    for copy in px_near + pg_in + px_other:
        copy().wait_recv()
    total = []
    for e in range(2):
        left = jnp.concatenate([pg[q, :, e * seg : e * seg + seg] for q in range(4)], axis=1)
        right = jnp.concatenate([px[q, e] for q in range(4)], axis=0)
        outer = jnp.dot(left, right, preferred_element_type=jnp.float32)
        total.append(outer * (1.0 / math.sqrt(LEN)))
    for t in range(16):
        r, c = 8 * (t // 2), 128 * (t % 2)
        msg[t] = jnp.concatenate(
            [total[0][r : r + 8, c : c + 128], total[1][r : r + 8, c : c + 128]], axis=0
        ).astype(jnp.bfloat16)

    here = 2 * z + yh
    msg_out, msg_in = exchange(
        lambda slot: msg.at[slot], dom_slot, here, plane_peers, msg_ss, msg_rs
    )
    for copy in msg_out:
        copy().start()
    dom_slot[here] = msg[here]
    for r in range(64):
        eg_ref[:, KX * r : KX * r + KX] = jnp.concatenate(
            [total[0][r : r + 1], total[1][r : r + 1]], axis=0
        ).astype(jnp.bfloat16)
    for copy in msg_in:
        copy().wait_recv()
    held = dom_slot[...].reshape(256, 128)
    domain_part = jnp.dot(hot, held, preferred_element_type=jnp.float32)

    sum_slot[x] = domain_part.astype(jnp.bfloat16)
    sum_out, sum_in = exchange(lambda slot: sum_slot.at[x], sum_slot, x, x_peers, sum_ss, sum_rs)
    for copy in sum_out:
        copy().start()
    for copy in sum_in:
        copy().wait_recv()
    share = sum(sum_slot[q].astype(jnp.float32) for q in range(4))
    own = jnp.concatenate([share[16 * r : 16 * r + 16] for r in range(8)], axis=1)
    high = own.astype(jnp.bfloat16).astype(jnp.float32)
    low = own - high
    left = jnp.concatenate([high, high, low], axis=1).astype(jnp.bfloat16)
    right = jnp.concatenate([high, low, high], axis=1)
    right = jnp.concatenate([right] * 8, axis=0).astype(jnp.bfloat16)
    wide = lax.dot_general(
        left, right, (((1,), (1,)), ((), ())), preferred_element_type=jnp.float32
    )
    on_diagonal = (
        lax.broadcasted_iota(jnp.int32, (16, 128), 1) // 16
        == lax.broadcasted_iota(jnp.int32, (16, 128), 0) % 8
    )
    wide = jnp.where(on_diagonal, wide, 0.0)
    flat = jnp.concatenate(
        [jnp.sum(wide[:8], axis=0, keepdims=True), jnp.sum(wide[8:], axis=0, keepdims=True)], axis=0
    )

    pending = px_out + forward + pg_out + msg_out + sum_out
    for slots, own_slot, peers, sends, receives in (
        (gram_c, 2 * y + core, column_peers, gc_ss, gc_rs),
        (gram_z, z, z_peers, gz_ss, gz_rs),
    ):
        slots[own_slot] = flat
        gram_out, gram_in = exchange(
            lambda slot: slots.at[own_slot], slots, own_slot, peers, sends, receives
        )
        for copy in gram_out:
            copy().start()
        for copy in pending:
            copy().wait_send()
        pending = gram_out
        for copy in gram_in:
            copy().wait_recv()
        flat = jnp.sum(slots[...], axis=0)
    for copy in pending:
        copy().wait_send()
    spread = jnp.concatenate(
        [jnp.broadcast_to(flat[0:1], (8, 128)), jnp.broadcast_to(flat[1:2], (8, 128))], axis=0
    )
    spread = jnp.where(on_diagonal, spread, 0.0)
    fold = (
        lax.broadcasted_iota(jnp.int32, (384, 16), 0) % 16
        == lax.broadcasted_iota(jnp.int32, (384, 16), 1)
    ).astype(jnp.bfloat16)
    high = spread.astype(jnp.bfloat16).astype(jnp.float32)
    middle = (spread - high).astype(jnp.bfloat16).astype(jnp.float32)
    pieces = jnp.concatenate([high, middle, spread - high - middle], axis=1).astype(jnp.bfloat16)
    out_ref[...] = jnp.dot(pieces, fold, preferred_element_type=jnp.float32) / (16.0 * KX * KG)


def keep(eg_ref, gram_ref, eg_out, gram_out):
    eg_out[...] = eg_ref[...]
    gram_out[...] = gram_ref[...]


def body(acts, grads, lengths, domains, hash_salts):
    ex_dev, seg, width_x = acts.shape
    width_g = grads.shape[2]
    tokens = ex_dev * seg
    chunks = (width_x + width_g) // PAIR
    rows = jnp.asarray(row_matrix(width_x // ROWS), jnp.bfloat16)
    dma = pltpu.SemaphoreType.DMA
    vmem = pl.BlockSpec(memory_space=pltpu.VMEM)
    results = (
        jax.ShapeDtypeStruct((ex_dev, 64 * KX), jnp.bfloat16),
        jax.ShapeDtypeStruct((DOMAINS, DOMAINS), jnp.float32),
    )
    made = pl.pallas_call(
        functools.partial(kernel, width_x, width_g),
        out_shape=results,
        in_specs=[
            pl.BlockSpec(memory_space=pltpu.SMEM),
            pl.BlockSpec(memory_space=pltpu.SMEM),
            pl.BlockSpec(memory_space=pl.ANY),
            pl.BlockSpec(memory_space=pl.ANY),
            vmem,
            vmem,
        ],
        out_specs=(vmem, vmem),
        scratch_shapes=[
            pltpu.VMEM((chunks, tokens, PAIR), jnp.bfloat16),
            pltpu.VMEM((2, PAIR, KX), jnp.bfloat16),
            pltpu.VMEM((2 * chunks, 128, KX), jnp.bfloat16),
            pltpu.VMEM((2, tokens, KX), jnp.float32),
            pltpu.VMEM((4, ex_dev, seg, KX), jnp.bfloat16),
            pltpu.VMEM((4, 64, tokens), jnp.bfloat16),
            pltpu.VMEM((4, 64, tokens), jnp.bfloat16),
            pltpu.VMEM((16, 16, 128), jnp.bfloat16),
            pltpu.VMEM((16, 16, 128), jnp.bfloat16),
            pltpu.VMEM((4, 128, 128), jnp.bfloat16),
            pltpu.VMEM((8, 2, 128), jnp.float32),
            pltpu.VMEM((8, 2, 128), jnp.float32),
            dma((chunks,)),
            dma((6,)),
            dma((4, 2)),
            dma((4,)),
            dma((4,)),
            dma((16,)),
            dma((16,)),
            dma((4,)),
            dma((4,)),
            dma((8,)),
            dma((8,)),
            dma((8,)),
            dma((8,)),
        ],
        compiler_params=pltpu.CompilerParams(
            collective_id=0, has_side_effects=True, vmem_limit_bytes=56 << 20
        ),
    )(
        lengths,
        hash_salts,
        acts.reshape(tokens, width_x),
        grads.reshape(tokens, width_g),
        rows,
        domains.reshape(1, domains.shape[0]),
    )
    return pl.pallas_call(keep, out_shape=results, in_specs=[vmem] * 2, out_specs=(vmem, vmem))(*made)


def solution(mesh):
    in_specs = (P("dp", "tok", None), P("dp", "tok", None), P("dp"), P(), P())
    out_specs = (P("dp", "tok"), P())
    return jax.shard_map(body, mesh=mesh, in_specs=in_specs, out_specs=out_specs, check_vma=False)
```
